32 devices in a mesh: prow: 4 (over y, core), pcol: 8 (over z, x).
Axes of the slice: x: 2, y: 2, z: 4, core: 2. Of those that a mesh axis runs over, the one named last changes fastest.
Arguments:
- cross_cov: float32 [2, 512, 16384], P(None, 'prow', 'pcol'), may hold values from -6 to 6
- prev_rows: bfloat16 [2, 512, 16384], P(None, 'pcol', 'prow'), may hold values from -0.0625 to 0.0625
- prev_solved: bfloat16 [16384, 16384], P('prow', 'pcol'), may hold values from -6 to 6
- sub_block: float32 [512, 512], replicated, may hold values from -0.25 to 0.25
- inv_first: float32 [512, 512], replicated, as said below
- inv_second: float32 [512, 512], replicated, as said below
Outputs:
- solved: float32 [2, 512, 16384], P(None, 'prow', 'pcol')
The draws below stay inside these ranges and needn't reach their ends.
Inputs may be any that keep to these rules, and one draw needn't show every extreme that they name: inv_first is lower triangular with a positive diagonal. inv_second is lower triangular with a positive diagonal.
All inputs are finite; a program needn't handle non-finite values.
Results may differ from the reference program's by a relative error of at most 0.0003.
Values may be sent and summed in bfloat16 or wider, within the bound.
No kernel may reach another device: no remote copies, remote signals or barrier semaphores. Data moves between devices by JAX's collectives and lax.ppermute only.
A program may use at most 128 MiB of HBM per device.

```python
import math
import jax
import jax.numpy as jnp
from jax import lax

NB = 512
R = 16384
PREV = 16384


def lower_inverse(key):
    first_key, second_key = jax.random.split(key)
    diagonal = jnp.exp(jax.random.uniform(first_key, (NB,), jnp.float32, math.log(0.5), math.log(2.0)))
    off_part = jax.random.normal(second_key, (NB, NB), jnp.float32)
    off_part = off_part * (1.0 / math.sqrt(NB))
    return jnp.tril(off_part, -1) + jnp.diag(diagonal)


def draw_inv_first(key, part):
    return lower_inverse(jax.random.fold_in(key, 11))


def draw_inv_second(key, part):
    return lower_inverse(jax.random.fold_in(key, 23))


def strengthened(result, key, source, target, blocks, factor):
    owner, partner = [(jnp.arange(result.shape[position]) // (result.shape[position] // blocks)).reshape([-1 if axis == position else 1 for axis in range(result.ndim)]) for position in (source, target)]
    chosen = jax.random.permutation(key, blocks)[partner]
    strong = (owner == chosen) | (owner == (partner + blocks // 2) % blocks)
    return jnp.where(strong, factor * result, result)


def level_of(stream_key, extent, pieces, least, top_value):
    factor_of = 1.0
    for dim, shards_of in pieces:
        draws = jax.random.uniform(jax.random.fold_in(jax.random.fold_in(stream_key, 6), dim), (shards_of,), jnp.float32, least / len(pieces), top_value / len(pieces))
        factor_of = factor_of * jnp.repeat(jnp.exp(draws), extent[dim] // shards_of).reshape((-1,) + (1,) * (len(extent) - 1 - dim))
    return factor_of


def bell_draw(rng, shape, width, limit, cuts=(), kind=jnp.bfloat16):
    values = jax.random.normal(rng, shape, jnp.float32) * width
    if len(cuts) > 0:
        values = level_of(rng, shape, cuts, -0.22, 0.18) * values
    return jnp.clip(values, min=-limit, max=limit).astype(kind)


def noise_with(stream_key, extent, scale, bound, shards, heavy, kind=jnp.bfloat16):
    drawn = scale * jax.random.normal(stream_key, extent, jnp.float32)
    if shards:
        drawn = drawn * level_of(stream_key, extent, shards, -0.22, 0.18)
    return jnp.clip(strengthened(drawn, jax.random.fold_in(stream_key, 3), *heavy), -bound, bound).astype(kind)


def setup_inputs(seed: int = 0) -> dict:
    seeds = jax.random.split(jax.random.key(seed), 7)
    return {
        "cross_cov": bell_draw(seeds[0], (2, NB, R), 1.0, 6.0, ((1, 4), (2, 8)), jnp.float32),
        "prev_rows": noise_with(seeds[1], (2, NB, PREV), PREV ** -0.5, 0.0625, ((1, 8), (2, 4)), (2, 1, 8, 2.0)),
        "prev_solved": bell_draw(seeds[2], (PREV, R), 1.0, 6.0, ((0, 4), (1, 8))),
        "sub_block": bell_draw(seeds[3], (NB, NB), NB ** -0.5, 0.25, (), jnp.float32),
        "inv_first": draw_inv_first(jax.random.fold_in(seeds[6], 71), 0),
        "inv_second": draw_inv_second(jax.random.fold_in(seeds[6], 71), 0),
    }


def mult(left, right):
    return jnp.dot(left, right, preferred_element_type=jnp.float32, precision=lax.Precision.HIGHEST)


def reference(cross_cov, prev_rows, prev_solved, sub_block, inv_first, inv_second):
    update_first = jnp.dot(prev_rows[0], prev_solved, preferred_element_type=jnp.float32)
    update_second = jnp.dot(prev_rows[1], prev_solved, preferred_element_type=jnp.float32)
    first_part = cross_cov[0] - update_first
    second_part = cross_cov[1] - update_second
    solved_first = mult(inv_first, first_part)
    second_rhs = second_part - mult(sub_block, solved_first)
    solved_second = mult(inv_second, second_rhs)
    return jnp.stack([solved_first, solved_second])
```

```python
import jax
import jax.numpy as jnp
from jax import lax
from jax.sharding import PartitionSpec as P


def mult(left, right, precision=lax.Precision.HIGH):
    return jnp.dot(left, right, preferred_element_type=jnp.float32, precision=precision)


def general(cross_cov, prev_rows, prev_solved, sub_block, inv_first, inv_second):
    terms = jnp.einsum(
        "kra,ac->krc",
        lax.all_gather(prev_rows, "pcol", axis=1, tiled=True),
        prev_solved,
        preferred_element_type=jnp.float32,
    )
    update = lax.psum_scatter(terms, "prow", scatter_dimension=1, tiled=True)
    reduced = lax.all_gather(cross_cov - update, "prow", axis=1, tiled=True)
    first = mult(inv_first, reduced[0], lax.Precision.HIGHEST)
    second = mult(inv_second, reduced[1] - mult(sub_block, first, lax.Precision.HIGHEST), lax.Precision.HIGHEST)
    rows = cross_cov.shape[1]
    return lax.dynamic_slice_in_dim(jnp.stack([first, second]), lax.axis_index("prow") * rows, rows, 1)


NZ, NX, NY, NC = 4, 2, 2, 2
SWAP_NEAR = [(q, q ^ NX) for q in range(NZ * NX)]
SWAP_MID = [(NX + x, 2 * NX + x) for x in range(NX)] + [(2 * NX + x, NX + x) for x in range(NX)]
OUTWARD = [(NX + x, x) for x in range(NX)] + [(2 * NX + x, 3 * NX + x) for x in range(NX)]
SWAP_X = [(q, q ^ 1) for q in range(NZ * NX)]
SWAP_CORE = [(p, p ^ 1) for p in range(NY * NC)]
SWAP_Y = [(p, p ^ NC) for p in range(NY * NC)]


def gather_panel(own, z):
    near = lax.ppermute(own, "pcol", SWAP_NEAR)
    own_x = lax.ppermute(own, "pcol", SWAP_X)
    near_x = lax.ppermute(near, "pcol", SWAP_X)
    mid = lax.ppermute(jnp.concatenate([own, near]), "pcol", SWAP_MID)
    edge = lax.ppermute(mid, "pcol", OUTWARD)
    far = jnp.where((z == 1) | (z == 2), mid, edge)
    far_x = lax.ppermute(far, "pcol", SWAP_X)
    return jnp.concatenate([own, near, own_x, near_x, far]), far_x


def fast(cross_cov, prev_rows, prev_solved, sub_block, inv_first, inv_second):
    p, q = lax.axis_index("prow"), lax.axis_index("pcol")
    z, x, y, core = q // NX, q % NX, p // NC, p % NC
    rows, block = cross_cov.shape[1], prev_rows.shape[1]
    size = NZ * NX * block

    low = z < 2
    f0, f1 = jnp.where(low, 2, 1), jnp.where(low, 3, 0)
    zs = [z, z ^ 1, z, z ^ 1, f0, f1, f0, f1]
    xs = [x, x, 1 - x, 1 - x, x, x, 1 - x, 1 - x]
    order = jnp.stack([a * NX + b for a, b in zip(zs, xs)])

    def arrived(matrix):
        return matrix.reshape(size, NZ * NX, block)[:, order].reshape(size, size)

    def own_columns(matrix):
        return lax.dynamic_slice_in_dim(matrix, p * rows, rows, 1)

    highest = lax.Precision.HIGHEST
    cross = -mult(inv_second, mult(sub_block, inv_first, highest), highest)
    base_first = mult(own_columns(inv_first), cross_cov[0])
    base_second = mult(own_columns(inv_second), cross_cov[1]) + mult(own_columns(cross), cross_cov[0])

    def terms(panel):
        early, last = gather_panel(prev_rows[panel], z)
        return jnp.concatenate([
            jnp.dot(early, prev_solved, preferred_element_type=jnp.float32),
            jnp.dot(last, prev_solved, preferred_element_type=jnp.float32),
        ])

    def summed(partial):
        partial = partial.reshape(NY, NC, rows, -1)
        pair = lax.dynamic_index_in_dim(partial, core, 1, False) + lax.ppermute(
            lax.dynamic_index_in_dim(partial, 1 - core, 1, False), "prow", SWAP_CORE)
        return lax.dynamic_index_in_dim(pair, y, 0, False) + lax.ppermute(
            lax.dynamic_index_in_dim(pair, 1 - y, 0, False), "prow", SWAP_Y)

    terms_first = terms(0)
    solved_first = summed(base_first - mult(arrived(inv_first), terms_first))
    base_second = base_second - mult(arrived(cross), terms_first)
    solved_second = summed(base_second - mult(arrived(inv_second), terms(1)))
    return jnp.stack([solved_first, solved_second])


def solution(mesh):
    sizes = dict(mesh.shape)
    return jax.shard_map(
        fast if (sizes["prow"], sizes["pcol"]) == (NY * NC, NZ * NX) else general,
        mesh=mesh,
        in_specs=(
            P(None, "prow", "pcol"),
            P(None, "pcol", "prow"),
            P("prow", "pcol"),
            P(),
            P(),
            P(),
        ),
        out_specs=P(None, "prow", "pcol"),
        check_vma=False,
    )
```

```python
import functools

import jax
import jax.numpy as jnp
from jax import lax
from jax.experimental import pallas as pl
from jax.experimental.pallas import tpu as pltpu
from jax.sharding import PartitionSpec as P

F32, BF16 = jnp.float32, jnp.bfloat16
COLS = 512
KERNEL_BYTES = 12 * 2**20
OCTAVES, LOWEST = 248.0, -124.0


def split(value):
    high = value.astype(BF16)
    return high, (value - high.astype(F32)).astype(BF16)


def dot(left, right):
    return jnp.dot(left, right, preferred_element_type=F32)


def products(starts_ref, piece_refs, rows_ref, solved_ref, columns):
    terms = dot(rows_ref[...], solved_ref[:, columns])
    top = 0
    for i, ref in enumerate(piece_refs):
        count = ref.shape[0]
        yield pl.ds(pl.multiple_of(starts_ref[i], 16), count), terms[top : top + count]
        top += count


def gather_rows(piece_refs, rows_ref):
    top = 0
    for ref in piece_refs:
        rows_ref[top : top + ref.shape[0]] = ref[...]
        top += ref.shape[0]


def chunks(ref, body):
    def step(j, carry):
        body(pl.ds(pl.multiple_of(j * COLS, COLS), COLS))
        return carry

    lax.fori_loop(0, ref.shape[1] // COLS, step, 0)


def early_kernel(starts_ref, *refs):
    *piece_refs, solved_ref, cov_ref, rhs_ref, rows_ref = refs
    n = len(piece_refs)
    gather_rows(piece_refs, rows_ref)

    def body(columns):
        rhs_ref[:, columns] = jnp.zeros((rhs_ref.shape[0], COLS), F32)
        rhs_ref[pl.ds(pl.multiple_of(starts_ref[n], 16), cov_ref.shape[0]), columns] = cov_ref[:, columns]
        for place, term in products(starts_ref, piece_refs, rows_ref, solved_ref, columns):
            rhs_ref[place, columns] = rhs_ref[place, columns] - term

    chunks(solved_ref, body)


def solve(pair_ref, high, low, top, count, end):
    size = high.shape[0]
    wide, fine = pair_ref[top : top + count, :end], pair_ref[size + top : size + top + count, :end]
    return dot(wide, high[:end]) + dot(wide, low[:end]) + dot(fine, high[:end])


def late_kernel(has_base, has_cross, devices, starts_ref, *refs):
    refs = list(refs)
    rows_ref, rhs_ref, out_ref = refs[-3:]
    n = len(refs) - 3 - 3 - 2 - has_base - 2 * has_cross
    piece_refs, refs = refs[:n], refs[n:-3]
    solved_ref, early_ref, pair_ref, *refs = refs
    keep_ref, send_ref = refs[-2:]
    size = early_ref.shape[0]
    block, count = size // 2, size // devices
    gather_rows(piece_refs, rows_ref)

    def body(columns):
        rhs_ref[...] = early_ref[:, columns]
        for place, term in products(starts_ref, piece_refs, rows_ref, solved_ref, columns):
            rhs_ref[place] = rhs_ref[place] - term
        high, low = split(rhs_ref[...])
        for top in (0, block):
            value = solve(pair_ref, high, low, top, block, top + block)
            if has_base:
                value = value + refs[0][top : top + block, columns]
            for at in range(0, block, count):
                place = pl.ds(pl.multiple_of(starts_ref[n + (top + at) // count], 16), count)
                out_ref[place] = value[at : at + count]
            if has_cross:
                refs[1][top : top + block, columns] = solve(refs[0], high, low, top, block, size)
        keep_ref[:, columns] = out_ref[:block]
        send_ref[:, columns] = out_ref[block:]

    chunks(solved_ref, body)


def call(kernel, starts, pieces, solved, full, outs, scratch, flops):
    depth, width = solved.shape
    rows = sum(piece.shape[0] for piece in pieces)
    vmem = pl.BlockSpec(memory_space=pltpu.VMEM)
    return pl.pallas_call(
        kernel,
        in_specs=[pl.BlockSpec(memory_space=pltpu.SMEM)] + [vmem] * (len(pieces) + 1 + len(full)),
        out_specs=[vmem] * len(outs),
        out_shape=[pltpu.VMEM((count, width), F32) for count in outs],
        scratch_shapes=[pltpu.VMEM((rows, depth), BF16)] + [pltpu.VMEM((count, COLS), F32) for count in scratch],
        compiler_params=pltpu.CompilerParams(vmem_limit_bytes=KERNEL_BYTES),
        cost_estimate=pl.CostEstimate(
            flops=2 * rows * depth * width + flops, bytes_accessed=2 * rows * depth, transcendentals=0
        ),
    )(starts, *pieces, solved, *full)


def hold_kernel(from_ref, to_ref, sems):
    copies = [
        pltpu.make_async_copy(from_ref.at[rows], to_ref.at[rows], sems.at[i])
        for i in range(sems.shape[0])
        for rows in [pl.ds(i * (from_ref.shape[0] // sems.shape[0]), from_ref.shape[0] // sems.shape[0])]
    ]
    for copy in copies:
        copy.start()
    for copy in copies:
        copy.wait()


def hold(array):
    return pl.pallas_call(
        hold_kernel,
        in_specs=[pl.BlockSpec(memory_space=pltpu.HBM)],
        out_specs=pl.BlockSpec(memory_space=pltpu.VMEM),
        out_shape=pltpu.VMEM(array.shape, array.dtype),
        scratch_shapes=[pltpu.SemaphoreType.DMA((4,))],
        compiler_params=pltpu.CompilerParams(vmem_limit_bytes=KERNEL_BYTES),
        cost_estimate=pl.CostEstimate(flops=0, bytes_accessed=2 * array.size, transcendentals=0),
    )(pltpu.with_memory_space_constraint(array, pltpu.HBM))


def pack_kernel(keep_ref, got_ref, own_ref, coded_ref):
    count = own_ref.shape[0]

    def body(columns):
        own_ref[:, columns] = keep_ref[:count, columns] + got_ref[:count, columns]
        value = keep_ref[count:, columns] + got_ref[count:, columns]
        size = jnp.abs(value)
        top = jnp.maximum(jnp.max(size, axis=0, keepdims=True) * 1.01, 1e-30).astype(BF16)
        level = jnp.minimum(size / top.astype(F32), 1.0) * OCTAVES + LOWEST
        coded = jnp.exp2(level)
        coded_ref[:count, columns] = jnp.where(value < 0, -coded, coded).astype(BF16)
        coded_ref[count:, columns] = jnp.broadcast_to(top, (coded_ref.shape[0] - count, COLS))

    chunks(keep_ref, body)


def pack(keep, got):
    width, count = keep.shape[1], keep.shape[0] // 2
    vmem = pl.BlockSpec(memory_space=pltpu.VMEM)
    return pl.pallas_call(
        pack_kernel,
        in_specs=[vmem] * 2,
        out_specs=[vmem] * 2,
        out_shape=[pltpu.VMEM((count, width), F32), pltpu.VMEM((count + 16, width), BF16)],
        compiler_params=pltpu.CompilerParams(vmem_limit_bytes=KERNEL_BYTES),
        cost_estimate=pl.CostEstimate(flops=10 * count * width, bytes_accessed=24 * count * width, transcendentals=count * width),
    )(keep, got)


def unpack_kernel(own0_ref, got0_ref, own1_ref, got1_ref, out_ref):
    cols = out_ref.shape[2]
    columns = pl.ds(pl.multiple_of(pl.program_id(0) * cols, cols), cols)
    for k, (own_ref, got_ref) in enumerate(((own0_ref, got0_ref), (own1_ref, got1_ref))):
        count = own_ref.shape[0]
        coded = got_ref[:count, columns].astype(F32)
        size = jnp.maximum(jnp.log2(jnp.abs(coded)) - LOWEST, 0.0) * (1.0 / OCTAVES)
        size = size * got_ref[count:, columns].astype(F32)[:1]
        out_ref[k] = own_ref[:, columns] + jnp.where(coded < 0, -size, size)


def unpack(own0, got0, own1, got1):
    count, width = own0.shape
    return pl.pallas_call(
        unpack_kernel,
        grid=(width // COLS,),
        in_specs=[pl.BlockSpec(memory_space=pltpu.VMEM)] * 4,
        out_specs=pl.BlockSpec((2, count, COLS), lambda j: (0, 0, j)),
        out_shape=jax.ShapeDtypeStruct((2, count, width), F32),
        compiler_params=pltpu.CompilerParams(vmem_limit_bytes=KERNEL_BYTES),
        cost_estimate=pl.CostEstimate(flops=20 * count * width, bytes_accessed=20 * count * width, transcendentals=2 * count * width),
    )(own0, got0, own1, got1)


def mult(left, right):
    return jnp.dot(left, right, preferred_element_type=F32, precision=lax.Precision.HIGHEST)


def general(cross_cov, prev_rows, prev_solved, sub_block, inv_first, inv_second):
    terms = jnp.einsum(
        "kra,ac->krc",
        lax.all_gather(prev_rows, "pcol", axis=1, tiled=True),
        prev_solved,
        preferred_element_type=F32,
    )
    update = lax.psum_scatter(terms, "prow", scatter_dimension=1, tiled=True)
    reduced = lax.all_gather(cross_cov - update, "prow", axis=1, tiled=True)
    first = mult(inv_first, reduced[0])
    second = mult(inv_second, reduced[1] - mult(sub_block, first))
    rows = cross_cov.shape[1]
    return lax.dynamic_slice_in_dim(jnp.stack([first, second]), lax.axis_index("prow") * rows, rows, 1)


RING = (0, 2, 4, 6, 7, 5, 3, 1)
N = len(RING)
AHEAD = [(RING[i], RING[(i + 1) % N]) for i in range(N)]
BACK = [(RING[(i + 1) % N], RING[i]) for i in range(N)]
DEVICES = 4
SWAP_CORE = [(p, p ^ 1) for p in range(DEVICES)]
SWAP_Y = [(p, p ^ 2) for p in range(DEVICES)]


def halves(matrix):
    high = lax.reduce_precision(matrix, 8, 7)
    return jnp.concatenate([high, matrix - high]).astype(BF16)


def after(value, *others):
    return lax.optimization_barrier((value, *others))[0]


def fast(cross_cov, prev_rows, prev_solved, sub_block, inv_first, inv_second):
    p, q = lax.axis_index("prow"), lax.axis_index("pcol")
    rows, block = cross_cov.shape[1], prev_rows.shape[1]
    half = block // 2
    spot = jnp.where(q % 2 == 0, q // 2, N - 1 - q // 2)

    def rows_of(steps, part=0):
        there = (spot + steps) % N
        return jnp.where(there < N // 2, 2 * there, 2 * (N - 1 - there) + 1) * block + part * half

    def ahead(x):
        return lax.ppermute(x, "pcol", AHEAD)

    def back(x):
        return lax.ppermute(x, "pcol", BACK)

    own_a, own_b = prev_rows[0], prev_rows[1]
    fa, ba, fb, bb = [own_a], [own_a], [own_b], [own_b]
    held = hold(prev_solved)
    for i in range(3):
        for f, b in ((fa, ba), (fb, bb)):
            f.append(ahead(after(f[-1], held) if i == 1 else f[-1]))
            b.append(back(b[-1]))
    for f, b in ((fa, ba), (fb, bb)):
        f.append(ahead(f[3][:half]))
        b.append(back(b[3][half:]))

    cross = -mult(inv_second, mult(sub_block, inv_first))

    slots = [((d % 2 != p % 2) * 2 + (d // 2 != p // 2)) * rows for d in range(DEVICES)]

    def starts(*values):
        return jnp.stack([jnp.asarray(v, jnp.int32) for v in values])

    own_cov = p * rows
    early_a = [own_a, fa[1], ba[1], fa[2], ba[2]]
    early_b = [own_b, fb[1], bb[1], fb[2], bb[2]]
    late_a = [fa[3], ba[3], fa[4], ba[4]]
    late_b = [fb[3], bb[3], fb[4], bb[4]]
    early_starts = starts(*[rows_of(s) for s in (0, -1, 1, -2, 2)], own_cov)
    late_starts = starts(rows_of(-3), rows_of(3), rows_of(4, 0), rows_of(4, 1), *slots)
    size = N * block

    solve_flops = 6 * size * size * cross_cov.shape[2]
    rhs_a, = call(early_kernel, early_starts, early_a, held, [cross_cov[0]], [size], [], 0)
    rhs_b, = call(early_kernel, early_starts, early_b, held, [cross_cov[1]], [size], [], 0)
    base, keep_a, send_a = call(
        functools.partial(late_kernel, 0, 1, DEVICES), late_starts, late_a, held,
        [rhs_a, halves(inv_first), halves(cross)], [size, size // 2, size // 2], [size, size], 2 * solve_flops)
    own0, coded = pack(keep_a, lax.ppermute(send_a, "prow", SWAP_CORE))
    got0 = lax.ppermute(coded, "prow", SWAP_Y)
    keep_b, send_b = call(
        functools.partial(late_kernel, 1, 0, DEVICES), late_starts, late_b, held,
        [rhs_b, halves(inv_second), base], [size // 2, size // 2], [size, size], solve_flops)
    own1, coded = pack(keep_b, lax.ppermute(send_b, "prow", SWAP_CORE))
    got1 = lax.ppermute(coded, "prow", SWAP_Y)
    return unpack(own0, got0, own1, got1)


def solution(mesh):
    sizes = dict(mesh.shape)
    return jax.shard_map(
        fast if (sizes["prow"], sizes["pcol"]) == (DEVICES, N) else general,
        mesh=mesh,
        in_specs=(
            P(None, "prow", "pcol"),
            P(None, "pcol", "prow"),
            P("prow", "pcol"),
            P(),
            P(),
            P(),
        ),
        out_specs=P(None, "prow", "pcol"),
        check_vma=False,
    )
```

```python
import functools

import jax
import jax.numpy as jnp
from jax import lax
from jax.experimental import pallas as pl
from jax.experimental.pallas import tpu as pltpu
from jax.sharding import PartitionSpec as P

F32, BF16 = jnp.float32, jnp.bfloat16
COLS, LANES = 512, 128
PIECES, SPLITS = 8, 2
COST = pl.CostEstimate(flops=0, bytes_accessed=0, transcendentals=0)
KERNEL_BYTES = 12 * 2**20
OCTAVES, LOWEST = 248.0, -124.0


VMEM = pl.BlockSpec(memory_space=pltpu.VMEM)


def params():
    return pltpu.CompilerParams(vmem_limit_bytes=KERNEL_BYTES)


def split(value):
    high = value.astype(BF16)
    return high, (value - high.astype(F32)).astype(BF16)


def dot(left, right):
    return jnp.dot(left, right, preferred_element_type=F32)


def products(starts_ref, piece_refs, rows_ref, solved_ref, columns):
    terms = dot(rows_ref[...], solved_ref[:, columns])
    top = 0
    for i, ref in enumerate(piece_refs):
        count = ref.shape[0]
        yield pl.ds(pl.multiple_of(starts_ref[i], 16), count), terms[top : top + count]
        top += count


def gather_rows(piece_refs, rows_ref):
    top = 0
    for ref in piece_refs:
        rows_ref[top : top + ref.shape[0]] = ref[...]
        top += ref.shape[0]


def early_kernel(streams, starts_ref, *refs):
    refs = list(refs)
    n = len(refs) - 4 - 2 * streams
    piece_refs, refs = refs[:n], refs[n:]
    if streams:
        solved_ref, cov_ref, rhs_ref, held_ref, rows_ref, sems = refs
    else:
        held_ref, cov_ref, rhs_ref, rows_ref = refs
    steps = held_ref.shape[1] // COLS
    spans = [slice(j * COLS, (j + 1) * COLS) for j in range(steps)]
    if streams:
        copies = [pltpu.make_async_copy(solved_ref.at[:, c], held_ref.at[:, c], sems.at[j]) for j, c in enumerate(spans)]
        copies[0].start()
        copies[1].start()
    gather_rows(piece_refs, rows_ref)
    for j, columns in enumerate(spans):
        if streams:
            copies[j].wait()
            if j + 2 < steps:
                copies[j + 2].start()
        rhs_ref[:, columns] = jnp.zeros((rhs_ref.shape[0], COLS), F32)
        rhs_ref[pl.ds(pl.multiple_of(starts_ref[n], 16), cov_ref.shape[0]), columns] = cov_ref[:, columns]
        for place, term in products(starts_ref, piece_refs, rows_ref, held_ref, columns):
            rhs_ref[place, columns] = rhs_ref[place, columns] - term


def early(starts, pieces, solved, cov, size, streams):
    depth, width = solved.shape
    rows = sum(piece.shape[0] for piece in pieces)
    scratch = [pltpu.VMEM((rows, depth), BF16)]
    outs = [pltpu.VMEM((size, width), F32)]
    if streams:
        solved = pltpu.with_memory_space_constraint(solved, pltpu.HBM)
        outs.append(pltpu.VMEM((depth, width), BF16))
        scratch.append(pltpu.SemaphoreType.DMA((width // COLS,)))
    return pl.pallas_call(
        functools.partial(early_kernel, streams),
        in_specs=[pl.BlockSpec(memory_space=pltpu.SMEM)]
        + [VMEM] * len(pieces)
        + [pl.BlockSpec(memory_space=pltpu.HBM) if streams else VMEM, VMEM],
        out_specs=[VMEM] * len(outs),
        out_shape=outs,
        scratch_shapes=scratch,
        compiler_params=params(),
        cost_estimate=COST,
    )(starts, *pieces, solved, cov)


def solve(pair_ref, high, low, top, count, end):
    size = high.shape[0]
    wide, fine = pair_ref[top : top + count, :end], pair_ref[size + top : size + top + count, :end]
    return dot(wide, high[:end]) + dot(wide, low[:end]) + dot(fine, high[:end])


def late_kernel(has_base, first, devices, starts_ref, *refs):
    refs = list(refs)
    n = len(refs) - 8 - PIECES
    piece_refs, refs = refs[:n], refs[n:]
    held_ref, early_ref, pair_ref = refs[:3]
    rows_ref, rhs_ref, out_ref = refs[-3:]
    if has_base:
        base_ref, keep_ref, *send_refs = refs[3:-3]
    else:
        keep_ref, *send_refs, whole_ref = refs[3:-3]
    size = early_ref.shape[0]
    block, count = size // 2, size // devices
    gather_rows(piece_refs, rows_ref)
    for j in range(keep_ref.shape[1] // COLS):
        here = slice(j * COLS, (j + 1) * COLS)
        columns = slice(first + j * COLS, first + (j + 1) * COLS)
        rhs_ref[...] = early_ref[:, columns]
        for place, term in products(starts_ref, piece_refs, rows_ref, held_ref, columns):
            rhs_ref[place] = rhs_ref[place] - term
        high, low = split(rhs_ref[...])
        if not has_base:
            whole_ref[:size, here] = high
            whole_ref[size:, here] = low
        for top in (0, block):
            value = solve(pair_ref, high, low, top, block, top + block)
            if has_base:
                value = value + base_ref[top : top + block, columns]
            for at in range(0, block, count):
                place = pl.ds(pl.multiple_of(starts_ref[n + (top + at) // count], 16), count)
                out_ref[place] = value[at : at + count]
        keep_ref[:, here] = out_ref[:block]
        for i, send_ref in enumerate(send_refs):
            few = block // PIECES
            send_ref[:, here] = out_ref[block + i * few : block + (i + 1) * few]


def late(starts, pieces, held, rhs, pair, base, first, width):
    depth = held.shape[0]
    rows, size = sum(piece.shape[0] for piece in pieces), rhs.shape[0]
    given = [held, rhs, pair] + ([] if base is None else [base])
    outs = [pltpu.VMEM((size // 2, width), F32)] + [pltpu.VMEM((size // 2 // PIECES, width), F32)] * PIECES
    if base is None:
        outs.append(pltpu.VMEM((2 * size, width), BF16))
    return pl.pallas_call(
        functools.partial(late_kernel, base is not None, first, DEVICES),
        in_specs=[pl.BlockSpec(memory_space=pltpu.SMEM)] + [VMEM] * (len(pieces) + len(given)),
        out_specs=[VMEM] * len(outs),
        out_shape=outs,
        scratch_shapes=[pltpu.VMEM((rows, depth), BF16)] + [pltpu.VMEM((size, COLS), F32)] * 2,
        compiler_params=params(),
        cost_estimate=COST,
    )(starts, *pieces, *given)


def times_kernel(pair_ref, whole_ref, out_ref):
    size = out_ref.shape[0]
    block = size // 2
    for j in range(out_ref.shape[1] // COLS):
        columns = slice(j * COLS, (j + 1) * COLS)
        for top in (0, block):
            out_ref[top : top + block, columns] = solve(
                pair_ref, whole_ref[:size, columns], whole_ref[size:, columns], top, block, size
            )


def times(pair, whole):
    size, width = whole.shape[0] // 2, whole.shape[1]
    return pl.pallas_call(
        times_kernel,
        in_specs=[VMEM] * 2,
        out_specs=VMEM,
        out_shape=pltpu.VMEM((size, width), F32),
        compiler_params=params(),
        cost_estimate=COST,
    )(pair, whole)


def pack_kernel(keep_ref, *refs):
    *got_refs, own_ref, coded_ref = refs
    count = own_ref.shape[0]
    near, far = got_refs[: PIECES // 2], got_refs[PIECES // 2 :]
    few = near[0].shape[0]
    for i, ref in enumerate(near):
        own_ref[i * few : (i + 1) * few] = keep_ref[i * few : (i + 1) * few] + ref[...]
    blocks = own_ref.shape[1] // LANES
    tops = []
    for i in range(blocks):
        columns = slice(i * LANES, (i + 1) * LANES)
        value = keep_ref[count:, columns] + jnp.concatenate([ref[:, columns] for ref in far])
        size = jnp.abs(value)
        top = jnp.maximum(jnp.max(size, axis=0, keepdims=True) * 1.01, 1e-30).astype(BF16)
        level = jnp.minimum(size / top.astype(F32), 1.0) * OCTAVES + LOWEST
        coded = jnp.exp2(level)
        coded_ref[i * count : (i + 1) * count] = jnp.where(value < 0, -coded, coded).astype(BF16)
        tops.append(top)
    tops.append(jnp.ones((coded_ref.shape[0] - blocks * (count + 1), LANES), BF16))
    coded_ref[blocks * count :] = jnp.concatenate([top for top in tops if top.shape[0]])


def pack(keep, got):
    width, count = keep.shape[1], keep.shape[0] // 2
    blocks = width // LANES
    return pl.pallas_call(
        pack_kernel,
        in_specs=[VMEM] * (1 + len(got)),
        out_specs=[VMEM] * 2,
        out_shape=[pltpu.VMEM((count, width), F32), pltpu.VMEM((blocks * count + -(-blocks // 16) * 16, LANES), BF16)],
        compiler_params=params(),
        cost_estimate=COST,
    )(keep, *got)


def unpack_kernel(*refs):
    *refs, out_ref = refs
    count = out_ref.shape[1]
    at = 0
    for own_ref, got_ref in zip(refs[::2], refs[1::2]):
        blocks = own_ref.shape[1] // LANES
        tops = got_ref[blocks * count :].astype(F32) * (1.0 / OCTAVES)
        for i in range(blocks):
            coded = got_ref[i * count : (i + 1) * count].astype(F32)
            size = jnp.maximum(jnp.log2(jnp.abs(coded)) - LOWEST, 0.0) * tops[i : i + 1]
            value = own_ref[:, i * LANES : (i + 1) * LANES] + jnp.where(coded < 0, -size, size)
            out_ref[at // out_ref.shape[2], :, at % out_ref.shape[2] : at % out_ref.shape[2] + LANES] = value
            at += LANES


def unpack(sums):
    count, width = sums[0][0].shape[0], sum(own.shape[1] for own, _ in sums) // 2
    return pl.pallas_call(
        unpack_kernel,
        in_specs=[VMEM] * (2 * len(sums)),
        out_specs=VMEM,
        out_shape=jax.ShapeDtypeStruct((2, count, width), F32),
        compiler_params=params(),
        cost_estimate=COST,
    )(*[array for pair in sums for array in pair])


def mult(left, right):
    return jnp.dot(left, right, preferred_element_type=F32, precision=lax.Precision.HIGHEST)


def general(cross_cov, prev_rows, prev_solved, sub_block, inv_first, inv_second):
    terms = jnp.einsum(
        "kra,ac->krc",
        lax.all_gather(prev_rows, "pcol", axis=1, tiled=True),
        prev_solved,
        preferred_element_type=F32,
    )
    update = lax.psum_scatter(terms, "prow", scatter_dimension=1, tiled=True)
    reduced = lax.all_gather(cross_cov - update, "prow", axis=1, tiled=True)
    first = mult(inv_first, reduced[0])
    second = mult(inv_second, reduced[1] - mult(sub_block, first))
    rows = cross_cov.shape[1]
    return lax.dynamic_slice_in_dim(jnp.stack([first, second]), lax.axis_index("prow") * rows, rows, 1)


RING = (0, 2, 4, 6, 7, 5, 3, 1)
N = len(RING)
AHEAD = [(RING[i], RING[(i + 1) % N]) for i in range(N)]
BACK = [(RING[(i + 1) % N], RING[i]) for i in range(N)]
DEVICES = 4
SWAP_CORE = [(p, p ^ 1) for p in range(DEVICES)]
SWAP_Y = [(p, p ^ 2) for p in range(DEVICES)]


def halves(matrix):
    high = lax.reduce_precision(matrix, 8, 7)
    return jnp.concatenate([high, matrix - high]).astype(BF16)


def after(value, *others):
    return lax.optimization_barrier((value, *others))[0]


def fast(cross_cov, prev_rows, prev_solved, sub_block, inv_first, inv_second):
    p, q = lax.axis_index("prow"), lax.axis_index("pcol")
    rows, block = cross_cov.shape[1], prev_rows.shape[1]
    half = block // 2
    spot = jnp.where(q % 2 == 0, q // 2, N - 1 - q // 2)

    def rows_of(steps, part=0):
        there = (spot + steps) % N
        return jnp.where(there < N // 2, 2 * there, 2 * (N - 1 - there) + 1) * block + part * half

    def starts(*values):
        return jnp.stack([jnp.asarray(v, jnp.int32) for v in values])

    size = N * block

    def ahead(x):
        return lax.ppermute(x, "pcol", AHEAD)

    def back(x):
        return lax.ppermute(x, "pcol", BACK)

    own_a, own_b = prev_rows[0], prev_rows[1]
    fa, ba, fb, bb = [own_a], [own_a], [own_b], [own_b]

    def step(flow, move, *others):
        flow.append(move(after(flow[-1], *others)))

    for f, b in ((fa, ba), (fb, bb), (fa, ba), (fb, bb), (fa, ba)):
        step(f, ahead)
        step(b, back)

    cross = -mult(inv_second, mult(sub_block, inv_first))

    slots = [((d % 2 != p % 2) * 2 + (d // 2 != p // 2)) * rows for d in range(DEVICES)]

    late_starts = starts(rows_of(-3), rows_of(3), rows_of(4, 0), rows_of(4, 1), *slots)
    matrices = [halves(inv_first), halves(cross), halves(inv_second)]
    early_starts = after(starts(*[rows_of(s) for s in (0, -1, 1, -2, 2)], p * rows), late_starts, *matrices)
    rhs_a, held = early(early_starts, [own_a, fa[1], ba[1], fa[2], ba[2]], prev_solved, cross_cov[0], size, True)
    step(fb, ahead, rhs_a)
    step(bb, back, rhs_a)
    fa.append(ahead(fa[3][:half]))
    ba.append(back(ba[3][half:]))
    rhs_b, = early(after(early_starts, fa[3], ba[3]), [own_b, fb[1], bb[1], fb[2], bb[2]], held, cross_cov[1], size, False)
    fb.append(ahead(after(fb[3], rhs_b)[:half]))
    bb.append(back(after(bb[3], rhs_b)[half:]))

    width = cross_cov.shape[2]

    def exchange(keep, sends, *others):
        return pack(after(keep, *others), [lax.ppermute(send, "prow", SWAP_CORE) for send in sends])

    keep, *sends, high_low = late(
        after(late_starts, rhs_b, fb[3], bb[3]), [fa[3], ba[3], fa[4], ba[4]], held, rhs_a, matrices[0], None, 0, width)
    sends = lax.optimization_barrier((*sends, fb[4], bb[4]))[:PIECES]
    base = times(matrices[1], high_low)
    own, coded = exchange(keep, sends, base)
    sums = [(own, lax.ppermute(coded, "prow", SWAP_Y))]
    ready = after(late_starts, coded)
    part = width // SPLITS
    for i in range(SPLITS):
        keep, *sends = late(ready, [fb[3], bb[3], fb[4], bb[4]], held, rhs_b, matrices[2], base, i * part, part)
        own, coded = exchange(keep, sends, *([sums[0][1]] if i == SPLITS - 1 else []))
        sums.append((own, lax.ppermute(coded, "prow", SWAP_Y)))
    return unpack(sums)


def solution(mesh):
    sizes = dict(mesh.shape)
    return jax.shard_map(
        fast if (sizes["prow"], sizes["pcol"]) == (DEVICES, N) else general,
        mesh=mesh,
        in_specs=(
            P(None, "prow", "pcol"),
            P(None, "pcol", "prow"),
            P("prow", "pcol"),
            P(),
            P(),
            P(),
        ),
        out_specs=P(None, "prow", "pcol"),
        check_vma=False,
    )
```

```python
import functools

import jax
import jax.numpy as jnp
from jax import lax
from jax.experimental import pallas as pl
from jax.experimental.pallas import tpu as pltpu
from jax.sharding import PartitionSpec as P

F32, BF16 = jnp.float32, jnp.bfloat16
COLS, LANES = 512, 128
PIECES, SPLITS = 4, 2
COST = pl.CostEstimate(flops=0, bytes_accessed=0, transcendentals=0)
KERNEL_BYTES = 12 * 2**20
OCTAVES, LOWEST = 248.0, -124.0


VMEM = pl.BlockSpec(memory_space=pltpu.VMEM)


def params():
    return pltpu.CompilerParams(vmem_limit_bytes=KERNEL_BYTES)


def split(value):
    high = value.astype(BF16)
    return high, (value - high.astype(F32)).astype(BF16)


def dot(left, right):
    return jnp.dot(left, right, preferred_element_type=F32)


def products(starts_ref, piece_refs, rows_ref, solved_ref, columns):
    terms = dot(rows_ref[...], solved_ref[:, columns])
    top = 0
    for i, ref in enumerate(piece_refs):
        count = ref.shape[0]
        yield pl.ds(pl.multiple_of(starts_ref[i], 16), count), terms[top : top + count]
        top += count


def gather_rows(piece_refs, rows_ref):
    top = 0
    for ref in piece_refs:
        rows_ref[top : top + ref.shape[0]] = ref[...]
        top += ref.shape[0]


def early_kernel(streams, starts_ref, *refs):
    refs = list(refs)
    n = len(refs) - 4 - 2 * streams
    piece_refs, refs = refs[:n], refs[n:]
    if streams:
        solved_ref, cov_ref, rhs_ref, held_ref, rows_ref, sems = refs
    else:
        held_ref, cov_ref, rhs_ref, rows_ref = refs
    steps = held_ref.shape[1] // COLS
    spans = [slice(j * COLS, (j + 1) * COLS) for j in range(steps)]
    if streams:
        copies = [pltpu.make_async_copy(solved_ref.at[:, c], held_ref.at[:, c], sems.at[j]) for j, c in enumerate(spans)]
        copies[0].start()
        copies[1].start()
    gather_rows(piece_refs, rows_ref)
    for j, columns in enumerate(spans):
        if streams:
            copies[j].wait()
            if j + 2 < steps:
                copies[j + 2].start()
        rhs_ref[:, columns] = jnp.zeros((rhs_ref.shape[0], COLS), F32)
        rhs_ref[pl.ds(pl.multiple_of(starts_ref[n], 16), cov_ref.shape[0]), columns] = cov_ref[:, columns]
        for place, term in products(starts_ref, piece_refs, rows_ref, held_ref, columns):
            rhs_ref[place, columns] = rhs_ref[place, columns] - term


def early(starts, pieces, solved, cov, size, streams):
    depth, width = solved.shape
    rows = sum(piece.shape[0] for piece in pieces)
    scratch = [pltpu.VMEM((rows, depth), BF16)]
    outs = [pltpu.VMEM((size, width), F32)]
    if streams:
        solved = pltpu.with_memory_space_constraint(solved, pltpu.HBM)
        outs.append(pltpu.VMEM((depth, width), BF16))
        scratch.append(pltpu.SemaphoreType.DMA((width // COLS,)))
    return pl.pallas_call(
        functools.partial(early_kernel, streams),
        in_specs=[pl.BlockSpec(memory_space=pltpu.SMEM)]
        + [VMEM] * len(pieces)
        + [pl.BlockSpec(memory_space=pltpu.HBM) if streams else VMEM, VMEM],
        out_specs=[VMEM] * len(outs),
        out_shape=outs,
        scratch_shapes=scratch,
        compiler_params=params(),
        cost_estimate=COST,
    )(starts, *pieces, solved, cov)


def solve(pair_ref, high, low, top, count, end):
    size = high.shape[0]
    wide, fine = pair_ref[top : top + count, :end], pair_ref[size + top : size + top + count, :end]
    return dot(wide, high[:end]) + dot(wide, low[:end]) + dot(fine, high[:end])


def late_kernel(has_base, first, devices, starts_ref, *refs):
    refs = list(refs)
    n = len(refs) - 8 - PIECES
    piece_refs, refs = refs[:n], refs[n:]
    held_ref, early_ref, pair_ref = refs[:3]
    rows_ref, rhs_ref, out_ref = refs[-3:]
    if has_base:
        base_ref, keep_ref, *send_refs = refs[3:-3]
    else:
        keep_ref, *send_refs, whole_ref = refs[3:-3]
    size = early_ref.shape[0]
    block, count = size // 2, size // devices
    gather_rows(piece_refs, rows_ref)
    for j in range(keep_ref.shape[1] // COLS):
        here = slice(j * COLS, (j + 1) * COLS)
        columns = slice(first + j * COLS, first + (j + 1) * COLS)
        rhs_ref[...] = early_ref[:, columns]
        for place, term in products(starts_ref, piece_refs, rows_ref, held_ref, columns):
            rhs_ref[place] = rhs_ref[place] - term
        high, low = split(rhs_ref[...])
        if not has_base:
            whole_ref[:size, here] = high
            whole_ref[size:, here] = low
        for top in (0, block):
            value = solve(pair_ref, high, low, top, block, top + block)
            if has_base:
                value = value + base_ref[top : top + block, columns]
            for at in range(0, block, count):
                place = pl.ds(pl.multiple_of(starts_ref[n + (top + at) // count], 16), count)
                out_ref[place] = value[at : at + count]
        keep_ref[:, here] = out_ref[:block]
        for i, send_ref in enumerate(send_refs):
            few = block // PIECES
            send_ref[:, here] = out_ref[block + i * few : block + (i + 1) * few]


def late(starts, pieces, held, rhs, pair, base, first, width):
    depth = held.shape[0]
    rows, size = sum(piece.shape[0] for piece in pieces), rhs.shape[0]
    given = [held, rhs, pair] + ([] if base is None else [base])
    outs = [pltpu.VMEM((size // 2, width), F32)] + [pltpu.VMEM((size // 2 // PIECES, width), F32)] * PIECES
    if base is None:
        outs.append(pltpu.VMEM((2 * size, width), BF16))
    return pl.pallas_call(
        functools.partial(late_kernel, base is not None, first, DEVICES),
        in_specs=[pl.BlockSpec(memory_space=pltpu.SMEM)] + [VMEM] * (len(pieces) + len(given)),
        out_specs=[VMEM] * len(outs),
        out_shape=outs,
        scratch_shapes=[pltpu.VMEM((rows, depth), BF16)] + [pltpu.VMEM((size, COLS), F32)] * 2,
        compiler_params=params(),
        cost_estimate=COST,
    )(starts, *pieces, *given)


def times_kernel(pair_ref, *refs):
    *whole_refs, out_ref = refs
    size = out_ref.shape[0]
    block, at = size // 2, 0
    for whole_ref in whole_refs:
        for j in range(whole_ref.shape[1] // COLS):
            here = slice(j * COLS, (j + 1) * COLS)
            for top in (0, block):
                out_ref[top : top + block, at : at + COLS] = solve(
                    pair_ref, whole_ref[:size, here], whole_ref[size:, here], top, block, size
                )
            at += COLS


def times(pair, wholes):
    size, width = wholes[0].shape[0] // 2, sum(whole.shape[1] for whole in wholes)
    return pl.pallas_call(
        times_kernel,
        in_specs=[VMEM] * (1 + len(wholes)),
        out_specs=VMEM,
        out_shape=pltpu.VMEM((size, width), F32),
        compiler_params=params(),
        cost_estimate=COST,
    )(pair, *wholes)


def pack_kernel(keep_ref, *refs):
    *got_refs, own_ref, coded_ref = refs
    count = own_ref.shape[0]
    near, far = got_refs[: PIECES // 2], got_refs[PIECES // 2 :]
    few = near[0].shape[0]
    for i, ref in enumerate(near):
        own_ref[i * few : (i + 1) * few] = keep_ref[i * few : (i + 1) * few] + ref[...]
    blocks = own_ref.shape[1] // LANES
    tops = []
    for i in range(blocks):
        columns = slice(i * LANES, (i + 1) * LANES)
        value = keep_ref[count:, columns] + jnp.concatenate([ref[:, columns] for ref in far])
        size = jnp.abs(value)
        top = jnp.maximum(jnp.max(size, axis=0, keepdims=True) * 1.01, 1e-30).astype(BF16)
        level = jnp.minimum(size / top.astype(F32), 1.0) * OCTAVES + LOWEST
        coded = jnp.exp2(level)
        coded_ref[i * count : (i + 1) * count] = jnp.where(value < 0, -coded, coded).astype(BF16)
        tops.append(top)
    tops.append(jnp.ones((coded_ref.shape[0] - blocks * (count + 1), LANES), BF16))
    coded_ref[blocks * count :] = jnp.concatenate([top for top in tops if top.shape[0]])


def pack(keep, got):
    width, count = keep.shape[1], keep.shape[0] // 2
    blocks = width // LANES
    return pl.pallas_call(
        pack_kernel,
        in_specs=[VMEM] * (1 + len(got)),
        out_specs=[VMEM] * 2,
        out_shape=[pltpu.VMEM((count, width), F32), pltpu.VMEM((blocks * count + -(-blocks // 16) * 16, LANES), BF16)],
        compiler_params=params(),
        cost_estimate=COST,
    )(keep, *got)


def unpack_kernel(*refs):
    *refs, out_ref = refs
    count = out_ref.shape[1]
    at = 0
    for own_ref, got_ref in zip(refs[::2], refs[1::2]):
        blocks = own_ref.shape[1] // LANES
        tops = got_ref[blocks * count :].astype(F32) * (1.0 / OCTAVES)
        for i in range(blocks):
            coded = got_ref[i * count : (i + 1) * count].astype(F32)
            size = jnp.maximum(jnp.log2(jnp.abs(coded)) - LOWEST, 0.0) * tops[i : i + 1]
            value = own_ref[:, i * LANES : (i + 1) * LANES] + jnp.where(coded < 0, -size, size)
            out_ref[at // out_ref.shape[2], :, at % out_ref.shape[2] : at % out_ref.shape[2] + LANES] = value
            at += LANES


def unpack(sums):
    count, width = sums[0][0].shape[0], sum(own.shape[1] for own, _ in sums) // 2
    return pl.pallas_call(
        unpack_kernel,
        in_specs=[VMEM] * (2 * len(sums)),
        out_specs=VMEM,
        out_shape=jax.ShapeDtypeStruct((2, count, width), F32),
        compiler_params=params(),
        cost_estimate=COST,
    )(*[array for pair in sums for array in pair])


def mult(left, right):
    return jnp.dot(left, right, preferred_element_type=F32, precision=lax.Precision.HIGHEST)


def general(cross_cov, prev_rows, prev_solved, sub_block, inv_first, inv_second):
    terms = jnp.einsum(
        "kra,ac->krc",
        lax.all_gather(prev_rows, "pcol", axis=1, tiled=True),
        prev_solved,
        preferred_element_type=F32,
    )
    update = lax.psum_scatter(terms, "prow", scatter_dimension=1, tiled=True)
    reduced = lax.all_gather(cross_cov - update, "prow", axis=1, tiled=True)
    first = mult(inv_first, reduced[0])
    second = mult(inv_second, reduced[1] - mult(sub_block, first))
    rows = cross_cov.shape[1]
    return lax.dynamic_slice_in_dim(jnp.stack([first, second]), lax.axis_index("prow") * rows, rows, 1)


RING = (0, 2, 4, 6, 7, 5, 3, 1)
N = len(RING)
AHEAD = [(RING[i], RING[(i + 1) % N]) for i in range(N)]
BACK = [(RING[(i + 1) % N], RING[i]) for i in range(N)]
DEVICES = 4
SWAP_CORE = [(p, p ^ 1) for p in range(DEVICES)]
SWAP_Y = [(p, p ^ 2) for p in range(DEVICES)]


def halves(matrix):
    high = lax.reduce_precision(matrix, 8, 7)
    return jnp.concatenate([high, matrix - high]).astype(BF16)


def after(value, *others):
    return lax.optimization_barrier((value, *others))[0]


def fast(cross_cov, prev_rows, prev_solved, sub_block, inv_first, inv_second):
    p, q = lax.axis_index("prow"), lax.axis_index("pcol")
    rows, block = cross_cov.shape[1], prev_rows.shape[1]
    half = block // 2
    spot = jnp.where(q % 2 == 0, q // 2, N - 1 - q // 2)

    def rows_of(steps, part=0):
        there = (spot + steps) % N
        return jnp.where(there < N // 2, 2 * there, 2 * (N - 1 - there) + 1) * block + part * half

    def starts(*values):
        return jnp.stack([jnp.asarray(v, jnp.int32) for v in values])

    size = N * block

    def ahead(x):
        return lax.ppermute(x, "pcol", AHEAD)

    def back(x):
        return lax.ppermute(x, "pcol", BACK)

    own_a, own_b = prev_rows[0], prev_rows[1]
    fa, ba, fb, bb = [own_a], [own_a], [own_b], [own_b]

    def step(flow, move, *others):
        flow.append(move(after(flow[-1], *others)))

    for f, b in ((fa, ba), (fb, bb), (fa, ba), (fb, bb), (fa, ba)):
        step(f, ahead)
        step(b, back)

    cross = -mult(inv_second, mult(sub_block, inv_first))

    slots = [((d % 2 != p % 2) * 2 + (d // 2 != p // 2)) * rows for d in range(DEVICES)]

    late_starts = starts(rows_of(-3), rows_of(3), rows_of(4, 0), rows_of(4, 1), *slots)
    matrices = [halves(inv_first), halves(cross), halves(inv_second)]
    early_starts = after(starts(*[rows_of(s) for s in (0, -1, 1, -2, 2)], p * rows), late_starts, *matrices)
    rhs_a, held = early(early_starts, [own_a, fa[1], ba[1], fa[2], ba[2]], prev_solved, cross_cov[0], size, True)
    rhs_b, = early(early_starts, [own_b, fb[1], bb[1], fb[2], bb[2]], held, cross_cov[1], size, False)
    fa.append(ahead(after(fa[3], rhs_b)[:half]))
    ba.append(back(after(ba[3], rhs_b)[half:]))
    step(fb, ahead, fa[4], ba[4])
    step(bb, back, fa[4], ba[4])
    fb.append(ahead(fb[3][:half]))
    bb.append(back(bb[3][half:]))

    width = cross_cov.shape[2]

    def exchange(keep, sends, *others):
        return pack(after(keep, *others), [lax.ppermute(send, "prow", SWAP_CORE) for send in sends])

    part = width // SPLITS
    last_a, last_b = [fa[3], ba[3], fa[4], ba[4]], [fb[3], bb[3], fb[4], bb[4]]
    sums, parts = [], []
    for i in range(SPLITS):
        keep, *sends, high_low = late(late_starts, last_a, held, rhs_a, matrices[0], None, i * part, part)
        own, coded = exchange(keep, sends, *([fb[3], bb[3]] if i else []))
        sums.append((own, lax.ppermute(coded, "prow", SWAP_Y)))
        parts.append(high_low)
    base = times(matrices[1], parts)
    for i in range(SPLITS):
        ready = after(late_starts, coded, *([sums[0][1]] if i else []))
        keep, *sends = late(ready, last_b, held, rhs_b, matrices[2], base, i * part, part)
        own, coded_b = exchange(keep, sends, *([sums[1][1]] if i else []))
        sums.append((own, lax.ppermute(coded_b, "prow", SWAP_Y)))
    return unpack(sums)


def solution(mesh):
    sizes = dict(mesh.shape)
    return jax.shard_map(
        fast if (sizes["prow"], sizes["pcol"]) == (DEVICES, N) else general,
        mesh=mesh,
        in_specs=(
            P(None, "prow", "pcol"),
            P(None, "pcol", "prow"),
            P("prow", "pcol"),
            P(),
            P(),
            P(),
        ),
        out_specs=P(None, "prow", "pcol"),
        check_vma=False,
    )
```

```python
import functools

import jax
import jax.numpy as jnp
from jax import lax
from jax.experimental import pallas as pl
from jax.experimental.pallas import tpu as pltpu
from jax.sharding import PartitionSpec as P

F32, BF16 = jnp.float32, jnp.bfloat16
COLS, LANES = 512, 128
PIECES, SPLITS = 4, 2
COST = pl.CostEstimate(flops=0, bytes_accessed=0, transcendentals=0)
KERNEL_BYTES = 10 * 2**20
OCTAVES, LOWEST = 248.0, -124.0


VMEM = pl.BlockSpec(memory_space=pltpu.VMEM)


def params():
    return pltpu.CompilerParams(vmem_limit_bytes=KERNEL_BYTES)


def split(value):
    high = value.astype(BF16)
    return high, (value - high.astype(F32)).astype(BF16)


def dot(left, right):
    return jnp.dot(left, right, preferred_element_type=F32)


def gather_rows(piece_refs, rows_ref):
    top = 0
    for ref in piece_refs:
        rows_ref[top : top + ref.shape[0]] = ref[...]
        top += ref.shape[0]


def by_spans(ref, body, unrolled=False):
    if unrolled:
        for start in range(0, ref.shape[1], COLS):
            body(start)
        return

    def step(j, carry):
        body(pl.multiple_of(j * COLS, COLS))
        return carry

    lax.fori_loop(0, ref.shape[1] // COLS, step, 0)


def take_off(starts_ref, piece_refs, rows_ref, held_ref, columns, rhs_ref):
    terms = dot(rows_ref[...], held_ref[:, columns])
    top = 0
    for i, ref in enumerate(piece_refs):
        count = ref.shape[0]
        place = pl.ds(pl.multiple_of(starts_ref[i], 16), count)
        rhs_ref[place, columns] = rhs_ref[place, columns] - terms[top : top + count]
        top += count


def first_kernel(n, starts_ref, *refs):
    pieces, (solved_ref, *refs) = refs[: 2 * n], refs[2 * n :]
    cov_refs, rhs_refs, (held_ref, rows_ref, sems) = refs[:2], refs[2:4], refs[4:]
    steps = held_ref.shape[1] // COLS

    def copy(j):
        columns = pl.ds(pl.multiple_of(j * COLS, COLS), COLS)
        return pltpu.make_async_copy(solved_ref.at[:, columns], held_ref.at[:, columns], sems.at[j])

    copy(0).start()
    copy(1).start()
    gather_rows(pieces, rows_ref)
    count, rows = pieces[0].shape[0], cov_refs[0].shape[0]

    def body(j, carry):
        columns = pl.ds(pl.multiple_of(j * COLS, COLS), COLS)
        for cov_ref, rhs_ref in zip(cov_refs, rhs_refs):
            rhs_ref[:, columns] = jnp.zeros((rhs_ref.shape[0], COLS), F32)
            rhs_ref[pl.ds(pl.multiple_of(starts_ref[n], 16), rows), columns] = cov_ref[:, columns]
        copy(j).wait()

        @pl.when(j + 2 < steps)
        def _():
            copy(j + 2).start()

        terms = dot(rows_ref[...], held_ref[:, columns])
        for i in range(2 * n):
            place = pl.ds(pl.multiple_of(starts_ref[i % n], 16), count)
            rhs_ref = rhs_refs[i // n]
            rhs_ref[place, columns] = rhs_ref[place, columns] - terms[i * count : (i + 1) * count]
        return carry

    lax.fori_loop(0, steps, body, 0)


def first(starts, pieces, solved, cov_a, cov_b, size):
    depth, width = solved.shape
    rows = sum(piece.shape[0] for piece in pieces)
    hbm = pl.BlockSpec(memory_space=pltpu.HBM)
    return pl.pallas_call(
        functools.partial(first_kernel, len(pieces) // 2),
        in_specs=[pl.BlockSpec(memory_space=pltpu.SMEM)] + [VMEM] * len(pieces) + [hbm, VMEM, VMEM],
        out_specs=[VMEM] * 3,
        out_shape=[pltpu.VMEM((size, width), F32)] * 2 + [pltpu.VMEM((depth, width), BF16)],
        scratch_shapes=[pltpu.VMEM((rows, depth), BF16), pltpu.SemaphoreType.DMA((width // COLS,))],
        compiler_params=params(),
        cost_estimate=COST,
    )(starts, *pieces, pltpu.with_memory_space_constraint(solved, pltpu.HBM), cov_a, cov_b)


def more_kernel(starts_ref, *refs):
    *piece_refs, held_ref, given_ref, rhs_ref, rows_ref = refs
    del given_ref
    gather_rows(piece_refs, rows_ref)

    def body(start):
        take_off(starts_ref, piece_refs, rows_ref, held_ref, pl.ds(start, COLS), rhs_ref)

    by_spans(held_ref, body)


def more(starts, pieces, held, rhs):
    rows = sum(piece.shape[0] for piece in pieces)
    return pl.pallas_call(
        more_kernel,
        in_specs=[pl.BlockSpec(memory_space=pltpu.SMEM)] + [VMEM] * (len(pieces) + 2),
        out_specs=VMEM,
        out_shape=pltpu.VMEM(rhs.shape, F32),
        input_output_aliases={len(pieces) + 2: 0},
        scratch_shapes=[pltpu.VMEM((rows, held.shape[0]), BF16)],
        compiler_params=params(),
        cost_estimate=COST,
    )(starts, *pieces, held, rhs)


def product(pair_ref, high, low, top, count, end):
    size = high.shape[0]
    wide, fine = pair_ref[top : top + count, :end], pair_ref[size + top : size + top + count, :end]
    return dot(wide, high[:end]) + dot(wide, low[:end]) + dot(fine, high[:end])


def solve_kernel(full, rhs_ref, pair_ref, *refs):
    *base_refs, out_ref = refs
    size, width = rhs_ref.shape
    block = size // 2

    def body(start):
        columns = pl.ds(start, COLS)
        high, low = split(rhs_ref[:, columns])
        for top in (0, block):
            place = slice(top, top + block)
            value = product(pair_ref, high, low, top, block, size if full else top + block)
            for base_ref in base_refs:
                value = value + base_ref[place, columns]
            out_ref[place, columns] = value

    by_spans(rhs_ref, body)


def solve(rhs, base, pair, full):
    given = [rhs, pair] + ([] if base is None else [base])
    return pl.pallas_call(
        functools.partial(solve_kernel, full),
        in_specs=[VMEM] * len(given),
        out_specs=[VMEM],
        out_shape=[pltpu.VMEM(rhs.shape, F32)],
        input_output_aliases={} if base is None else {2: 0},
        compiler_params=params(),
        cost_estimate=COST,
    )(*given)


def last_kernel(n, sends, at, starts_ref, *refs):
    refs = list(refs)
    piece_refs, refs = refs[:n], refs[n:]
    held_ref, sum_ref, matrix_ref, *refs = refs
    *refs, rows_ref, stack_ref, out_ref = refs
    keep_ref, *send_refs = refs[: sends + 1]
    parts_refs = refs[sends + 1 :]
    size = sum_ref.shape[0]
    block, count = size // 2, size // DEVICES
    few = block // sends
    gather_rows(piece_refs, rows_ref)
    rows = rows_ref.shape[0]

    def body(start):
        here, columns = pl.ds(start, COLS), pl.ds(at + start, COLS)
        high, low = split(dot(rows_ref[...], held_ref[:, columns]))
        for k, part in enumerate((high, low, high)):
            stack_ref[k * rows : (k + 1) * rows] = part
        for parts_ref in parts_refs:
            parts_ref[:, here] = stack_ref[...]
        value = sum_ref[:, columns] - dot(matrix_ref[...], stack_ref[...])
        for d in range(DEVICES):
            out_ref[pl.ds(pl.multiple_of(starts_ref[d], 16), count)] = value[d * count : (d + 1) * count]
        keep_ref[:, here] = out_ref[:block]
        for i, send_ref in enumerate(send_refs):
            send_ref[:, here] = out_ref[block + i * few : block + (i + 1) * few]

    by_spans(keep_ref, body, True)


def last(starts, pieces, held, total, matrix, at, width, sends, gives_parts):
    depth = held.shape[0]
    rows, size = sum(piece.shape[0] for piece in pieces), total.shape[0]
    given = [held, total, matrix]
    outs = [pltpu.VMEM((size // 2, width), F32)] + [pltpu.VMEM((size // 2 // sends, width), F32)] * sends
    if gives_parts:
        outs.append(pltpu.VMEM((3 * rows, width), BF16))
    return pl.pallas_call(
        functools.partial(last_kernel, len(pieces), sends, at),
        in_specs=[pl.BlockSpec(memory_space=pltpu.SMEM)] + [VMEM] * (len(pieces) + len(given)),
        out_specs=[VMEM] * len(outs),
        out_shape=outs,
        scratch_shapes=[
            pltpu.VMEM((rows, depth), BF16),
            pltpu.VMEM((matrix.shape[1], COLS), BF16),
            pltpu.VMEM((size, COLS), F32),
        ],
        compiler_params=params(),
        cost_estimate=COST,
    )(starts, *pieces, *given)


def less_kernel(sum_ref, matrix_ref, *refs):
    *part_refs, out_ref = refs
    at = 0
    for part_ref in part_refs:

        def body(start, part_ref=part_ref, at=at):
            columns = pl.ds(at + start, COLS)
            out_ref[:, columns] = sum_ref[:, columns] - dot(matrix_ref[...], part_ref[:, pl.ds(start, COLS)])

        by_spans(part_ref, body, True)
        at += part_ref.shape[1]


def less(total, matrix, parts):
    return pl.pallas_call(
        less_kernel,
        in_specs=[VMEM] * (2 + len(parts)),
        out_specs=VMEM,
        out_shape=pltpu.VMEM(total.shape, F32),
        input_output_aliases={0: 0},
        compiler_params=params(),
        cost_estimate=COST,
    )(total, matrix, *parts)


def pack_kernel(parts, *refs):
    *refs, own_ref, coded_ref = refs
    count = own_ref.shape[0]
    blocks = own_ref.shape[1] // LANES
    tops, block = [], 0
    for i in range(parts):
        keep_ref, *got_refs = refs[i * len(refs) // parts : (i + 1) * len(refs) // parts]
        near, far = got_refs[: len(got_refs) // 2], got_refs[len(got_refs) // 2 :]
        few, width = near[0].shape
        for k, ref in enumerate(near):
            rows = slice(k * few, (k + 1) * few)
            own_ref[rows, block * LANES : block * LANES + width] = keep_ref[rows] + ref[...]
        for start in range(0, width, LANES):
            columns = slice(start, start + LANES)
            value = keep_ref[count:, columns] + jnp.concatenate([ref[:, columns] for ref in far])
            size = jnp.abs(value)
            top = jnp.maximum(jnp.max(size, axis=0, keepdims=True) * 1.01, 1e-30).astype(BF16)
            level = jnp.minimum(size / top.astype(F32), 1.0) * OCTAVES + LOWEST
            coded = jnp.exp2(level)
            coded_ref[block * count : (block + 1) * count] = jnp.where(value < 0, -coded, coded).astype(BF16)
            tops.append(top)
            block += 1
    spare = coded_ref.shape[0] - blocks * (count + 1)
    if spare:
        tops.append(jnp.ones((spare, LANES), BF16))
    coded_ref[blocks * count :] = jnp.concatenate(tops)


def pack(parts):
    count, width = parts[0][0].shape[0] // 2, sum(keep.shape[1] for keep, _ in parts)
    blocks = width // LANES
    given = [array for keep, got in parts for array in (keep, *got)]
    return pl.pallas_call(
        functools.partial(pack_kernel, len(parts)),
        in_specs=[VMEM] * len(given),
        out_specs=[VMEM] * 2,
        out_shape=[pltpu.VMEM((count, width), F32), pltpu.VMEM((blocks * count + -(-blocks // 16) * 16, LANES), BF16)],
        compiler_params=params(),
        cost_estimate=COST,
    )(*given)


def unpack_kernel(*refs):
    *refs, out_ref = refs
    count = out_ref.shape[1]
    at = 0
    for own_ref, got_ref in zip(refs[::2], refs[1::2]):
        blocks = own_ref.shape[1] // LANES
        tops = got_ref[blocks * count :].astype(F32) * (1.0 / OCTAVES)
        for i in range(blocks):
            coded = got_ref[i * count : (i + 1) * count].astype(F32)
            size = jnp.maximum(jnp.log2(jnp.abs(coded)) - LOWEST, 0.0) * tops[i : i + 1]
            value = own_ref[:, i * LANES : (i + 1) * LANES] + jnp.where(coded < 0, -size, size)
            out_ref[at // out_ref.shape[2], :, at % out_ref.shape[2] : at % out_ref.shape[2] + LANES] = value
            at += LANES


def unpack(sums):
    count, width = sums[0][0].shape[0], sum(own.shape[1] for own, _ in sums) // 2
    return pl.pallas_call(
        unpack_kernel,
        in_specs=[VMEM] * (2 * len(sums)),
        out_specs=VMEM,
        out_shape=jax.ShapeDtypeStruct((2, count, width), F32),
        compiler_params=params(),
        cost_estimate=COST,
    )(*[array for pair in sums for array in pair])


def mult(left, right):
    return jnp.dot(left, right, preferred_element_type=F32, precision=lax.Precision.HIGHEST)


def general(cross_cov, prev_rows, prev_solved, sub_block, inv_first, inv_second):
    terms = jnp.einsum(
        "kra,ac->krc",
        lax.all_gather(prev_rows, "pcol", axis=1, tiled=True),
        prev_solved,
        preferred_element_type=F32,
    )
    update = lax.psum_scatter(terms, "prow", scatter_dimension=1, tiled=True)
    reduced = lax.all_gather(cross_cov - update, "prow", axis=1, tiled=True)
    first = mult(inv_first, reduced[0])
    second = mult(inv_second, reduced[1] - mult(sub_block, first))
    rows = cross_cov.shape[1]
    return lax.dynamic_slice_in_dim(jnp.stack([first, second]), lax.axis_index("prow") * rows, rows, 1)


RING = (0, 2, 4, 6, 7, 5, 3, 1)
N = len(RING)
AHEAD = [(RING[i], RING[(i + 1) % N]) for i in range(N)]
BACK = [(RING[(i + 1) % N], RING[i]) for i in range(N)]
DEVICES = 4
SWAP_CORE = [(p, p ^ 1) for p in range(DEVICES)]
SWAP_Y = [(p, p ^ 2) for p in range(DEVICES)]


def halves(matrix):
    high = lax.reduce_precision(matrix, 8, 7)
    return jnp.concatenate([high, matrix - high]).astype(BF16)


def after(value, *others):
    return lax.optimization_barrier((value, *others))[0]


def fast(cross_cov, prev_rows, prev_solved, sub_block, inv_first, inv_second):
    p, q = lax.axis_index("prow"), lax.axis_index("pcol")
    rows, block = cross_cov.shape[1], prev_rows.shape[1]
    half = block // 2
    spot = jnp.where(q % 2 == 0, q // 2, N - 1 - q // 2)

    def rows_of(steps, part=0):
        there = (spot + steps) % N
        return jnp.where(there < N // 2, 2 * there, 2 * (N - 1 - there) + 1) * block + part * half

    def starts(*values):
        return jnp.stack([jnp.asarray(v, jnp.int32) for v in values])

    size = N * block

    def ahead(x):
        return lax.ppermute(x, "pcol", AHEAD)

    def back(x):
        return lax.ppermute(x, "pcol", BACK)

    own_a, own_b = prev_rows[0], prev_rows[1]
    fa, ba, fb, bb = [own_a], [own_a], [own_b], [own_b]

    def step(flow, move, *others):
        flow.append(move(after(flow[-1], *others)))

    for f, b in ((fa, ba), (fb, bb)):
        step(f, ahead)
        step(b, back)

    cross = -mult(inv_second, mult(sub_block, inv_first))
    matrices = [halves(inv_first), halves(cross), halves(inv_second)]
    rest = jnp.concatenate([rows_of(steps) + jnp.arange(block) for steps in (-3, 3, 4)])
    chosen = jnp.arange(size)[:, None] == rest[None]
    columns = [dot(matrix, chosen.astype(BF16)).astype(BF16) for matrix in matrices]
    columns = [jnp.concatenate([c[:size], c[:size], c[size:]], 1) for c in columns]
    slots = starts(*[((d % 2 != p % 2) * 2 + (d // 2 != p // 2)) * rows for d in range(DEVICES)])
    place = starts(rows_of(-2), rows_of(2))
    first_place = after(starts(rows_of(0), rows_of(-1), rows_of(1), p * rows), slots, place, *columns, *matrices)

    step(fa, ahead)
    step(ba, back)
    step(fb, ahead)
    step(bb, back)
    known = [own_a, fa[1], ba[1], own_b, fb[1], bb[1]]
    rhs_a, rhs_b, held = first(first_place, known, prev_solved, cross_cov[0], cross_cov[1], size)
    step(fa, ahead, held)
    step(ba, back, held)
    rhs_a = more(place, [fa[2], ba[2]], held, rhs_a)
    sum_a, = solve(rhs_a, None, matrices[0], False)
    base, = solve(rhs_a, None, matrices[1], True)
    rhs_b = more(after(place, sum_a, base), [fb[2], bb[2]], held, rhs_b)
    fa.append(ahead(after(fa[3], rhs_b)[:half]))
    ba.append(back(after(ba[3], rhs_b)[half:]))
    sum_b, = solve(after(rhs_b, fa[3], ba[3]), base, matrices[2], False)
    step(fb, ahead, fa[4], ba[4], sum_b)
    step(bb, back, fa[4], ba[4], sum_b)
    fb.append(ahead(fb[3][:half]))
    bb.append(back(bb[3][half:]))
    last_b = [fb[3], bb[3], fb[4], bb[4]]

    width = cross_cov.shape[2]

    def across(sends):
        return [lax.ppermute(send, "prow", SWAP_CORE) for send in sends]

    part = width // SPLITS
    halves_a, parts = [], []
    for i in range(SPLITS):
        ready = after(slots, sum_b)
        keep, *sends, given = last(ready, [fa[3], ba[3], fa[4], ba[4]], held, sum_a, columns[0], i * part, part, PIECES, True)
        halves_a.append((keep, across(sends)))
        parts.append(given)
    sum_b = less(sum_b, columns[1], parts)
    keep, got = halves_a[0]
    halves_a[0] = after(keep, fb[3], bb[3]), got
    own, coded = pack(halves_a)
    sums = [(own, lax.ppermute(coded, "prow", SWAP_Y))]
    for i in range(SPLITS):
        keep, *sends = last(after(slots, coded), last_b, held, sum_b, columns[2], i * part, part, PIECES, False)
        own, coded = pack([(after(keep, *([got for _, got in sums] if i else [])), across(sends))])
        sums.append((own, lax.ppermute(coded, "prow", SWAP_Y)))
    return unpack(sums)


def solution(mesh):
    sizes = dict(mesh.shape)
    return jax.shard_map(
        fast if (sizes["prow"], sizes["pcol"]) == (DEVICES, N) else general,
        mesh=mesh,
        in_specs=(
            P(None, "prow", "pcol"),
            P(None, "pcol", "prow"),
            P("prow", "pcol"),
            P(),
            P(),
            P(),
        ),
        out_specs=P(None, "prow", "pcol"),
        check_vma=False,
    )
```

```python
import functools

import jax
import jax.numpy as jnp
from jax import lax
from jax.experimental import pallas as pl
from jax.experimental.pallas import tpu as pltpu
from jax.sharding import PartitionSpec as P

F32, BF16 = jnp.float32, jnp.bfloat16
COLS, LANES = 512, 128
PIECES, SPLITS = 4, 2
COST = pl.CostEstimate(flops=0, bytes_accessed=0, transcendentals=0)
KERNEL_BYTES = 10 * 2**20
OCTAVES, LOWEST = 248.0, -124.0


VMEM = pl.BlockSpec(memory_space=pltpu.VMEM)


def params():
    return pltpu.CompilerParams(vmem_limit_bytes=KERNEL_BYTES)


def split(value):
    high = value.astype(BF16)
    return high, (value - high.astype(F32)).astype(BF16)


def dot(left, right):
    return jnp.dot(left, right, preferred_element_type=F32)


def gather_rows(piece_refs, rows_ref):
    top = 0
    for ref in piece_refs:
        rows_ref[top : top + ref.shape[0]] = ref[...]
        top += ref.shape[0]


def by_spans(ref, body, unrolled=False):
    if unrolled:
        for start in range(0, ref.shape[1], COLS):
            body(start)
        return

    def step(j, carry):
        body(pl.multiple_of(j * COLS, COLS))
        return carry

    lax.fori_loop(0, ref.shape[1] // COLS, step, 0)


def take_off(starts_ref, piece_refs, rows_ref, held_ref, columns, rhs_ref):
    terms = dot(rows_ref[...], held_ref[:, columns])
    top = 0
    for i, ref in enumerate(piece_refs):
        count = ref.shape[0]
        place = pl.ds(pl.multiple_of(starts_ref[i], 16), count)
        rhs_ref[place, columns] = rhs_ref[place, columns] - terms[top : top + count]
        top += count


def first_kernel(n, starts_ref, *refs):
    pieces, (solved_ref, *refs) = refs[: 2 * n], refs[2 * n :]
    cov_refs, rhs_refs, (held_ref, rows_ref, sems) = refs[:2], refs[2:4], refs[4:]
    steps = held_ref.shape[1] // COLS

    def copy(j):
        columns = pl.ds(pl.multiple_of(j * COLS, COLS), COLS)
        return pltpu.make_async_copy(solved_ref.at[:, columns], held_ref.at[:, columns], sems.at[j])

    copy(0).start()
    copy(1).start()
    gather_rows(pieces, rows_ref)
    count, rows = pieces[0].shape[0], cov_refs[0].shape[0]

    def body(j, carry):
        columns = pl.ds(pl.multiple_of(j * COLS, COLS), COLS)
        for cov_ref, rhs_ref in zip(cov_refs, rhs_refs):
            rhs_ref[:, columns] = jnp.zeros((rhs_ref.shape[0], COLS), F32)
            rhs_ref[pl.ds(pl.multiple_of(starts_ref[n], 16), rows), columns] = cov_ref[:, columns]
        copy(j).wait()

        @pl.when(j + 2 < steps)
        def _():
            copy(j + 2).start()

        terms = dot(rows_ref[...], held_ref[:, columns])
        for i in range(2 * n):
            place = pl.ds(pl.multiple_of(starts_ref[i % n], 16), count)
            rhs_ref = rhs_refs[i // n]
            rhs_ref[place, columns] = rhs_ref[place, columns] - terms[i * count : (i + 1) * count]
        return carry

    lax.fori_loop(0, steps, body, 0)


def first(starts, pieces, solved, cov_a, cov_b, size):
    depth, width = solved.shape
    rows = sum(piece.shape[0] for piece in pieces)
    hbm = pl.BlockSpec(memory_space=pltpu.HBM)
    return pl.pallas_call(
        functools.partial(first_kernel, len(pieces) // 2),
        in_specs=[pl.BlockSpec(memory_space=pltpu.SMEM)] + [VMEM] * len(pieces) + [hbm, VMEM, VMEM],
        out_specs=[VMEM] * 3,
        out_shape=[pltpu.VMEM((size, width), F32)] * 2 + [pltpu.VMEM((depth, width), BF16)],
        scratch_shapes=[pltpu.VMEM((rows, depth), BF16), pltpu.SemaphoreType.DMA((width // COLS,))],
        compiler_params=params(),
        cost_estimate=COST,
    )(starts, *pieces, pltpu.with_memory_space_constraint(solved, pltpu.HBM), cov_a, cov_b)


def more_kernel(starts_ref, *refs):
    *piece_refs, held_ref, given_ref, rhs_ref, rows_ref = refs
    del given_ref
    gather_rows(piece_refs, rows_ref)

    def body(start):
        take_off(starts_ref, piece_refs, rows_ref, held_ref, pl.ds(start, COLS), rhs_ref)

    by_spans(held_ref, body)


def more(starts, pieces, held, rhs):
    rows = sum(piece.shape[0] for piece in pieces)
    return pl.pallas_call(
        more_kernel,
        in_specs=[pl.BlockSpec(memory_space=pltpu.SMEM)] + [VMEM] * (len(pieces) + 2),
        out_specs=VMEM,
        out_shape=pltpu.VMEM(rhs.shape, F32),
        input_output_aliases={len(pieces) + 2: 0},
        scratch_shapes=[pltpu.VMEM((rows, held.shape[0]), BF16)],
        compiler_params=params(),
        cost_estimate=COST,
    )(starts, *pieces, held, rhs)


def product(pair_ref, high, low, top, count, end):
    size = high.shape[0]
    wide, fine = pair_ref[top : top + count, :end], pair_ref[size + top : size + top + count, :end]
    return dot(wide, high[:end]) + dot(wide, low[:end]) + dot(fine, high[:end])


def solve_kernel(full, rhs_ref, pair_ref, *refs):
    *base_refs, out_ref = refs
    size, width = rhs_ref.shape
    block = size // 2

    def body(start):
        columns = pl.ds(start, COLS)
        high, low = split(rhs_ref[:, columns])
        for top in (0, block):
            place = slice(top, top + block)
            value = product(pair_ref, high, low, top, block, size if full else top + block)
            for base_ref in base_refs:
                value = value + base_ref[place, columns]
            out_ref[place, columns] = value

    by_spans(rhs_ref, body)


def solve(rhs, base, pair, full):
    given = [rhs, pair] + ([] if base is None else [base])
    return pl.pallas_call(
        functools.partial(solve_kernel, full),
        in_specs=[VMEM] * len(given),
        out_specs=[VMEM],
        out_shape=[pltpu.VMEM(rhs.shape, F32)],
        input_output_aliases={} if base is None else {2: 0},
        compiler_params=params(),
        cost_estimate=COST,
    )(*given)


def last_kernel(n, sends, at, starts_ref, *refs):
    refs = list(refs)
    piece_refs, refs = refs[:n], refs[n:]
    held_ref, sum_ref, matrix_ref, *refs = refs
    *refs, rows_ref, stack_ref, out_ref = refs
    keep_ref, *send_refs = refs[: sends + 1]
    parts_refs = refs[sends + 1 :]
    size = sum_ref.shape[0]
    block, count = size // 2, size // DEVICES
    few = block // sends
    gather_rows(piece_refs, rows_ref)
    rows = rows_ref.shape[0]

    def body(start):
        here, columns = pl.ds(start, COLS), pl.ds(at + start, COLS)
        high, low = split(dot(rows_ref[...], held_ref[:, columns]))
        for k, part in enumerate((high, low, high)):
            stack_ref[k * rows : (k + 1) * rows] = part
        for parts_ref in parts_refs:
            parts_ref[:, here] = stack_ref[...]
        value = sum_ref[:, columns] - dot(matrix_ref[...], stack_ref[...])
        for d in range(DEVICES):
            out_ref[pl.ds(pl.multiple_of(starts_ref[d], 16), count)] = value[d * count : (d + 1) * count]
        keep_ref[:, here] = out_ref[:block]
        for i, send_ref in enumerate(send_refs):
            send_ref[:, here] = out_ref[block + i * few : block + (i + 1) * few]

    by_spans(keep_ref, body, True)


def last(starts, pieces, held, total, matrix, at, width, sends, gives_parts):
    depth = held.shape[0]
    rows, size = sum(piece.shape[0] for piece in pieces), total.shape[0]
    given = [held, total, matrix]
    outs = [pltpu.VMEM((size // 2, width), F32)] + [pltpu.VMEM((size // 2 // sends, width), F32)] * sends
    if gives_parts:
        outs.append(pltpu.VMEM((3 * rows, width), BF16))
    return pl.pallas_call(
        functools.partial(last_kernel, len(pieces), sends, at),
        in_specs=[pl.BlockSpec(memory_space=pltpu.SMEM)] + [VMEM] * (len(pieces) + len(given)),
        out_specs=[VMEM] * len(outs),
        out_shape=outs,
        scratch_shapes=[
            pltpu.VMEM((rows, depth), BF16),
            pltpu.VMEM((matrix.shape[1], COLS), BF16),
            pltpu.VMEM((size, COLS), F32),
        ],
        compiler_params=params(),
        cost_estimate=COST,
    )(starts, *pieces, *given)


def less_kernel(sum_ref, matrix_ref, *refs):
    *part_refs, out_ref = refs
    at = 0
    for part_ref in part_refs:

        def body(start, part_ref=part_ref, at=at):
            columns = pl.ds(at + start, COLS)
            out_ref[:, columns] = sum_ref[:, columns] - dot(matrix_ref[...], part_ref[:, pl.ds(start, COLS)])

        by_spans(part_ref, body, True)
        at += part_ref.shape[1]


def less(total, matrix, parts):
    return pl.pallas_call(
        less_kernel,
        in_specs=[VMEM] * (2 + len(parts)),
        out_specs=VMEM,
        out_shape=pltpu.VMEM(total.shape, F32),
        input_output_aliases={0: 0},
        compiler_params=params(),
        cost_estimate=COST,
    )(total, matrix, *parts)


def pack_kernel(parts, *refs):
    *refs, own_ref, coded_ref = refs
    count = own_ref.shape[0]
    blocks = own_ref.shape[1] // LANES
    tops, block = [], 0
    for i in range(parts):
        keep_ref, *got_refs = refs[i * len(refs) // parts : (i + 1) * len(refs) // parts]
        near, far = got_refs[: len(got_refs) // 2], got_refs[len(got_refs) // 2 :]
        few, width = near[0].shape
        for k, ref in enumerate(near):
            rows = slice(k * few, (k + 1) * few)
            own_ref[rows, block * LANES : block * LANES + width] = keep_ref[rows] + ref[...]
        for start in range(0, width, LANES):
            columns = slice(start, start + LANES)
            value = keep_ref[count:, columns] + jnp.concatenate([ref[:, columns] for ref in far])
            size = jnp.abs(value)
            top = jnp.maximum(jnp.max(size, axis=0, keepdims=True) * 1.01, 1e-30).astype(BF16)
            level = jnp.minimum(size / top.astype(F32), 1.0) * OCTAVES + LOWEST
            coded = jnp.exp2(level)
            coded_ref[block * count : (block + 1) * count] = jnp.where(value < 0, -coded, coded).astype(BF16)
            tops.append(top)
            block += 1
    spare = coded_ref.shape[0] - blocks * (count + 1)
    if spare:
        tops.append(jnp.ones((spare, LANES), BF16))
    coded_ref[blocks * count :] = jnp.concatenate(tops)


def pack(parts):
    count, width = parts[0][0].shape[0] // 2, sum(keep.shape[1] for keep, _ in parts)
    blocks = width // LANES
    given = [array for keep, got in parts for array in (keep, *got)]
    return pl.pallas_call(
        functools.partial(pack_kernel, len(parts)),
        in_specs=[VMEM] * len(given),
        out_specs=[VMEM] * 2,
        out_shape=[pltpu.VMEM((count, width), F32), pltpu.VMEM((blocks * count + -(-blocks // 16) * 16, LANES), BF16)],
        compiler_params=params(),
        cost_estimate=COST,
    )(*given)


def unpack_kernel(panel, first, own_ref, got_ref, *refs):
    *_, out_ref, value_ref, sems = refs
    count, width = own_ref.shape
    blocks = width // LANES
    tops = got_ref[blocks * count :].astype(F32) * (1.0 / OCTAVES)
    copies = []
    for i in range(blocks):
        coded = got_ref[i * count : (i + 1) * count].astype(F32)
        size = jnp.maximum(jnp.log2(jnp.abs(coded)) - LOWEST, 0.0) * tops[i : i + 1]
        columns = slice(i * LANES, (i + 1) * LANES)
        value_ref[:, columns] = own_ref[:, columns] + jnp.where(coded < 0, -size, size)
        if (i + 1) * LANES % COLS == 0:
            done = slice((i + 1) * LANES - COLS, (i + 1) * LANES)
            there = out_ref.at[panel, :, first + done.start : first + done.stop]
            copies.append(pltpu.make_async_copy(value_ref.at[:, done], there, sems.at[len(copies)]))
            copies[-1].start()
    for copy in copies:
        copy.wait()


def unpack(sums):
    count, width = sums[0][0].shape[0], sum(own.shape[1] for own, _ in sums) // 2
    hbm = pl.BlockSpec(memory_space=pltpu.HBM)
    out, at = [], 0
    for own, got in sums:
        out = [
            pl.pallas_call(
                functools.partial(unpack_kernel, at // width, at % width),
                in_specs=[VMEM] * 2 + [hbm] * len(out),
                out_specs=hbm,
                out_shape=jax.ShapeDtypeStruct((2, count, width), F32),
                input_output_aliases={2: 0} if out else {},
                scratch_shapes=[pltpu.VMEM(own.shape, F32), pltpu.SemaphoreType.DMA((own.shape[1] // COLS,))],
                compiler_params=params(),
                cost_estimate=COST,
            )(own, got, *out)
        ]
        at += own.shape[1]
    return out[0]


def mult(left, right):
    return jnp.dot(left, right, preferred_element_type=F32, precision=lax.Precision.HIGHEST)


def general(cross_cov, prev_rows, prev_solved, sub_block, inv_first, inv_second):
    terms = jnp.einsum(
        "kra,ac->krc",
        lax.all_gather(prev_rows, "pcol", axis=1, tiled=True),
        prev_solved,
        preferred_element_type=F32,
    )
    update = lax.psum_scatter(terms, "prow", scatter_dimension=1, tiled=True)
    reduced = lax.all_gather(cross_cov - update, "prow", axis=1, tiled=True)
    first = mult(inv_first, reduced[0])
    second = mult(inv_second, reduced[1] - mult(sub_block, first))
    rows = cross_cov.shape[1]
    return lax.dynamic_slice_in_dim(jnp.stack([first, second]), lax.axis_index("prow") * rows, rows, 1)


RING = (0, 2, 4, 6, 7, 5, 3, 1)
N = len(RING)
AHEAD = [(RING[i], RING[(i + 1) % N]) for i in range(N)]
BACK = [(RING[(i + 1) % N], RING[i]) for i in range(N)]
DEVICES = 4
SWAP_CORE = [(p, p ^ 1) for p in range(DEVICES)]
SWAP_Y = [(p, p ^ 2) for p in range(DEVICES)]


def halves(matrix):
    high = lax.reduce_precision(matrix, 8, 7)
    return jnp.concatenate([high, matrix - high]).astype(BF16)


def after(value, *others):
    return lax.optimization_barrier((value, *others))[0]


def fast(cross_cov, prev_rows, prev_solved, sub_block, inv_first, inv_second):
    p, q = lax.axis_index("prow"), lax.axis_index("pcol")
    rows, block = cross_cov.shape[1], prev_rows.shape[1]
    half = block // 2
    spot = jnp.where(q % 2 == 0, q // 2, N - 1 - q // 2)

    def rows_of(steps, part=0):
        there = (spot + steps) % N
        return jnp.where(there < N // 2, 2 * there, 2 * (N - 1 - there) + 1) * block + part * half

    def starts(*values):
        return jnp.stack([jnp.asarray(v, jnp.int32) for v in values])

    size = N * block

    def ahead(x):
        return lax.ppermute(x, "pcol", AHEAD)

    def back(x):
        return lax.ppermute(x, "pcol", BACK)

    own_a, own_b = prev_rows[0], prev_rows[1]
    fa, ba, fb, bb = [own_a], [own_a], [own_b], [own_b]

    def step(flow, move, *others):
        flow.append(move(after(flow[-1], *others)))

    for f, b in ((fa, ba), (fb, bb)):
        step(f, ahead)
        step(b, back)

    cross = -mult(inv_second, mult(sub_block, inv_first))
    matrices = [halves(inv_first), halves(cross), halves(inv_second)]
    rest = jnp.concatenate([rows_of(steps) + jnp.arange(block) for steps in (-3, 3, 4)])
    chosen = jnp.arange(size)[:, None] == rest[None]
    columns = [dot(matrix, chosen.astype(BF16)).astype(BF16) for matrix in matrices]
    columns = [jnp.concatenate([c[:size], c[:size], c[size:]], 1) for c in columns]
    slots = starts(*[((d % 2 != p % 2) * 2 + (d // 2 != p // 2)) * rows for d in range(DEVICES)])
    place = starts(rows_of(-2), rows_of(2))
    first_place = after(starts(rows_of(0), rows_of(-1), rows_of(1), p * rows), slots, place, *columns, *matrices)

    step(fa, ahead)
    step(ba, back)
    step(fb, ahead)
    step(bb, back)
    known = [own_a, fa[1], ba[1], own_b, fb[1], bb[1]]
    rhs_a, rhs_b, held = first(first_place, known, prev_solved, cross_cov[0], cross_cov[1], size)
    step(fa, ahead, held)
    step(ba, back, held)
    rhs_a = more(place, [fa[2], ba[2]], held, rhs_a)
    sum_a, = solve(rhs_a, None, matrices[0], False)
    base, = solve(rhs_a, None, matrices[1], True)
    rhs_b = more(after(place, sum_a, base), [fb[2], bb[2]], held, rhs_b)
    fa.append(ahead(after(fa[3], rhs_b)[:half]))
    ba.append(back(after(ba[3], rhs_b)[half:]))
    sum_b, = solve(after(rhs_b, fa[3], ba[3]), base, matrices[2], False)
    step(fb, ahead, fa[4], ba[4], sum_b)
    step(bb, back, fa[4], ba[4], sum_b)
    fb.append(ahead(fb[3][:half]))
    bb.append(back(bb[3][half:]))
    last_b = [fb[3], bb[3], fb[4], bb[4]]

    width = cross_cov.shape[2]

    def across(sends):
        return [lax.ppermute(send, "prow", SWAP_CORE) for send in sends]

    part = width // SPLITS
    halves_a, parts = [], []
    for i in range(SPLITS):
        ready = after(slots, sum_b)
        keep, *sends, given = last(ready, [fa[3], ba[3], fa[4], ba[4]], held, sum_a, columns[0], i * part, part, PIECES, True)
        halves_a.append((keep, across(sends)))
        parts.append(given)
    sum_b = less(sum_b, columns[1], parts)
    keep, got = halves_a[0]
    halves_a[0] = after(keep, fb[3], bb[3]), got
    own, coded = pack(halves_a)
    sums = [(own, lax.ppermute(coded, "prow", SWAP_Y))]
    at = 0
    for i, (wide, sends) in enumerate(((3 * width // 4, 2 * PIECES), (width // 4, PIECES))):
        keep, *sends = last(after(slots, coded), last_b, held, sum_b, columns[2], at, wide, sends, False)
        own, coded = pack([(after(keep, *([sums[0][1]] if i else [])), across(sends))])
        sums.append((own, lax.ppermute(coded, "prow", SWAP_Y)))
        at += wide
    return unpack(sums)


def solution(mesh):
    sizes = dict(mesh.shape)
    return jax.shard_map(
        fast if (sizes["prow"], sizes["pcol"]) == (DEVICES, N) else general,
        mesh=mesh,
        in_specs=(
            P(None, "prow", "pcol"),
            P(None, "pcol", "prow"),
            P("prow", "pcol"),
            P(),
            P(),
            P(),
        ),
        out_specs=P(None, "prow", "pcol"),
        check_vma=False,
    )
```
